32 devices in a mesh: blk: 8 (over z, x), col: 4 (over y, core).
Axes of the slice: x: 2, y: 2, z: 4, core: 2. Of those that a mesh axis runs over, the one named last changes fastest.
Arguments:
- upper_row: float32 [512, 8, 512], P(None, 'blk', 'col'), may hold values from -0.17 to 4.17, as said below
- lower_row: float32 [512, 8, 512], P(None, 'blk', 'col'), may hold values from -0.1 to 0.1
Outputs:
- new_upper: float32 [512, 8, 512], P(None, 'blk', 'col')
- new_lower: float32 [512, 8, 512], P(None, 'blk', 'col')
The draws below stay inside these ranges and needn't reach their ends.
Inputs may be any that keep to these rules, and one draw needn't show every extreme that they name: Block 0 of upper_row is 4 times the identity plus entries within 0.16 of it; the other blocks hold entries within 0.1.
All inputs are finite; a program needn't handle non-finite values.
Results may differ from the reference program's by a relative error of at most 0.00023.
Values sent between devices are 32-bit elements; how exact they have to be, the bound alone decides.
No kernel may reach another device: no remote copies, remote signals or barrier semaphores. Data moves between devices by JAX's collectives and lax.ppermute only.
A program may use at most 64 MiB of HBM per device.

```python
import jax
import jax.numpy as jnp
from jax import lax

BLOCK = 512
STEPS = 1
NBLK = 8


def draw_upper_row(key, part):
    shape_all = (BLOCK, NBLK, BLOCK)
    noise_draw = jnp.clip(jax.random.normal(key, shape_all, jnp.float32), -4.0, 4.0)
    leading = (jnp.arange(NBLK) == 0).astype(jnp.float32)[None, :, None]
    spread = 0.025 + 0.015 * leading
    diagonal = (jnp.arange(BLOCK)[:, None] == jnp.arange(BLOCK)[None, :]).astype(jnp.float32)
    return noise_draw * spread + 4.0 * diagonal[:, None, :] * leading


def draw_lower_row(key, part):
    shape_all = (BLOCK, NBLK, BLOCK)
    noise_key = jax.random.fold_in(key, 11)
    noise_draw = jnp.clip(jax.random.normal(noise_key, shape_all, jnp.float32), -4.0, 4.0)
    return noise_draw * 0.025


def setup_inputs(seed: int = 0) -> dict:
    key_list = jax.random.split(jax.random.key(seed), 3)
    upper_row = draw_upper_row(jax.random.fold_in(key_list[2], 71), 0)
    lower_row = draw_lower_row(jax.random.fold_in(key_list[2], 71), 0)
    return {"upper_row": upper_row, "lower_row": lower_row}


HIGHEST_PREC = lax.Precision.HIGHEST

def product(left_mat, right_mat):
    return jnp.dot(left_mat, right_mat, precision=HIGHEST_PREC, preferred_element_type=jnp.float32)

def inverse_root(matrix, identity):
    first_term = (3.0 * identity - matrix) / 2.0
    second_term = (3.0 * identity - product(matrix, product(first_term, first_term))) / 2.0
    return product(first_term, second_term)

def reference(upper_row, lower_row):
    identity = jnp.eye(BLOCK, dtype=jnp.float32)
    upper_flat = upper_row.reshape(BLOCK, NBLK * BLOCK)
    lower_flat = lower_row.reshape(BLOCK, NBLK * BLOCK)
    for step_index in range(1, STEPS + 1):
        upper_flat = jnp.concatenate([jnp.zeros((BLOCK, BLOCK), jnp.float32), upper_flat[:, :-BLOCK]], axis=1)
        head_upper = upper_flat[:, step_index * BLOCK:(step_index + 1) * BLOCK]
        head_lower = lower_flat[:, step_index * BLOCK:(step_index + 1) * BLOCK]
        norm_scale = jnp.sqrt(jnp.sum(head_upper * head_upper) / BLOCK + 1e-06)
        inverse_one = (2.0 * identity - head_upper / norm_scale) / norm_scale
        inverse_two = product(inverse_one, 2.0 * identity - product(head_upper, inverse_one))
        reflect = product(head_lower, inverse_two)
        left_root = inverse_root(identity - product(reflect.T, reflect), identity)
        right_root = inverse_root(identity - product(reflect, reflect.T), identity)
        next_upper = product(left_root, upper_flat - product(reflect.T, lower_flat))
        next_lower = product(right_root, lower_flat - product(reflect, upper_flat))
        upper_flat, lower_flat = (next_upper, next_lower)
    return (upper_flat.reshape(BLOCK, NBLK, BLOCK), lower_flat.reshape(BLOCK, NBLK, BLOCK))
```

```python
import functools

import jax
import jax.numpy as jnp
from jax import lax
from jax.experimental import pallas as pl
from jax.experimental.pallas import tpu as pltpu
from jax.sharding import PartitionSpec as P

PAIR = 2


def halves(value):
    high = value.astype(jnp.bfloat16)
    return high, (value - high.astype(jnp.float32)).astype(jnp.bfloat16)


def product(left, right, contract=(1, 0)):
    (left_high, left_low), (right_high, right_low) = left, right
    return lax.dot_general(
        jnp.concatenate([left_high, left_high, left_low], axis=contract[0]),
        jnp.concatenate([right_high, right_low, right_high], axis=contract[1]),
        (((contract[0],), (contract[1],)), ((), ())),
        preferred_element_type=jnp.float32,
    )


def step_kernel(groups, place_ref, *refs):
    count = groups * PAIR
    shares = refs[: PAIR * count]
    upper_ref, lower_ref, new_upper_ref, new_lower_ref = refs[PAIR * count : PAIR * count + 4]
    head_ref, rest_high, rest_low, low_high, low_low = refs[PAIR * count + 4 :]
    order, width = upper_ref.shape
    on_upper = place_ref[0] == 0
    total = jnp.zeros((8, width), jnp.float32)
    for step in range(groups):
        for side in range(PAIR):
            group = lax.rem(place_ref[1] + step, groups)
            column = group * PAIR + lax.rem(place_ref[2] + side, PAIR)
            same = shares[step * PAIR + side][...]
            other = shares[count + step * PAIR + side][...]
            head = jnp.where(on_upper, same, other)
            head_ref[column] = head
            total = total + jnp.sum((head * head).reshape(-1, 8, width), axis=0)
            low_high[column], low_low[column] = halves(jnp.where(on_upper, other, same))
    scale = lax.rsqrt(jnp.sum(total) / order + 1e-06)
    rows = lax.broadcasted_iota(jnp.int32, (order, width), 0)
    lanes = lax.broadcasted_iota(jnp.int32, (order, width), 1)
    for column in range(count):
        identity = jnp.where(rows == lanes + column * width, 1.0, 0.0)
        rest_high[column], rest_low[column] = halves(identity - head_ref[column] * scale)

    def joined(ref):
        return jnp.concatenate([ref[column] for column in range(count)], axis=1)

    rest = (joined(rest_high), joined(rest_low))
    low = (joined(low_high), joined(low_low))
    square = halves(product(rest, rest))
    middle = low[0].astype(jnp.float32) + low[1].astype(jnp.float32) + product(low, rest)
    reflect = halves((middle + product(halves(middle), square)) * scale)
    upper = upper_ref[...]
    lower = lower_ref[...]
    gram = halves(product(reflect, reflect, (1, 1)))
    mixed = upper - product(reflect, halves(lower), (0, 0))
    residue = lower - product(reflect, halves(upper))
    both = jnp.concatenate([product(reflect, halves(mixed)), product(gram, halves(residue))], axis=1)
    inner = 0.3125 * both + 0.0625 * product(gram, halves(both))
    inner = 0.375 * both + product(gram, halves(inner))
    inner = 0.5 * both + product(gram, halves(inner))
    new_upper_ref[...] = mixed + product(reflect, halves(inner[:, :width]), (0, 0))
    new_lower_ref[...] = residue + inner[:, width:]


def step_call(place, shares, upper, lower, groups):
    order, width = upper.shape
    count = groups * PAIR
    whole = pl.BlockSpec(memory_space=pltpu.VMEM)
    return pl.pallas_call(
        functools.partial(step_kernel, groups),
        out_shape=(jax.ShapeDtypeStruct(upper.shape, jnp.float32),) * 2,
        in_specs=[pl.BlockSpec(memory_space=pltpu.SMEM)] + [whole] * (len(shares) + 2),
        out_specs=(whole, whole),
        scratch_shapes=[pltpu.VMEM((count, order, width), jnp.float32)]
        + [pltpu.VMEM((count, order, width), jnp.bfloat16)] * 4,
        compiler_params=pltpu.CompilerParams(vmem_limit_bytes=48 * 1024 * 1024),
    )(place, *shares, upper, lower)


def spread(share, rows, row):
    stride = 1
    while stride < rows:
        stride *= 2
    while stride > 1:
        stride //= 2
        pairs = [(first, first + stride) for first in range(0, rows - stride, 2 * stride)]
        sends = [(PAIR * a + x, PAIR * b + x) for a, b in pairs for x in range(PAIR)]
        received = lax.ppermute(share, "blk", sends)
        share = jnp.where(lax.rem(row, 2 * stride) == stride, received, share)
    return share


def exchange(share, rows, groups):
    size = groups * PAIR
    shares = []
    for flip in range(PAIR):
        for step in range(groups):
            sends = [
                (
                    (PAIR * row + (x ^ flip)) * size + (y + step) % groups * PAIR + core,
                    (PAIR * row + x) * size + y * PAIR + core,
                )
                for row in range(rows)
                for x in range(PAIR)
                for y in range(groups)
                for core in range(PAIR)
            ]
            mine = lax.ppermute(share, ("blk", "col"), sends) if flip or step else share
            swap = [(column, column ^ 1) for column in range(size)]
            shares += [mine, lax.ppermute(mine, "col", swap)]
    return shares


def shards(upper_row, lower_row):
    blocks, size = lax.axis_size("blk"), lax.axis_size("col")
    assert upper_row.shape[1] == 1 and blocks % PAIR == 0 and size % PAIR == 0
    rows, groups = blocks // PAIR, size // PAIR
    block, column = lax.axis_index("blk"), lax.axis_index("col")
    upper, lower = upper_row[:, 0, :], lower_row[:, 0, :]
    shifted = lax.ppermute(upper, "blk", [(source, source + 1) for source in range(blocks - 1)])
    side = lax.rem(block, PAIR)
    share = spread(jnp.where(side == 0, upper, lower), rows, block // PAIR)
    shares = exchange(share, rows, groups)
    place = jnp.stack([side, column // PAIR, lax.rem(column, PAIR)]).astype(jnp.int32)
    new_upper, new_lower = step_call(place, shares, shifted, lower, groups)
    return new_upper[:, None, :], new_lower[:, None, :]


def solution(mesh):
    placement = P(None, "blk", "col")
    return jax.shard_map(
        shards,
        mesh=mesh,
        in_specs=(placement, placement),
        out_specs=(placement, placement),
        check_vma=False,
    )
```

```python
import functools

import jax
import jax.numpy as jnp
from jax import lax
from jax.experimental import pallas as pl
from jax.experimental.pallas import tpu as pltpu
from jax.sharding import PartitionSpec as P

PAIR = 2
LEAD = 4.0


def halves(value):
    high = value.astype(jnp.bfloat16)
    return high, (value - high.astype(jnp.float32)).astype(jnp.bfloat16)


def whole(parts):
    return parts[0].astype(jnp.float32) + parts[1].astype(jnp.float32)


def product(left, right, side=0):
    (left_high, left_low), (right_high, right_low) = left, right
    return lax.dot_general(
        jnp.concatenate([left_high, left_high, left_low], axis=1),
        jnp.concatenate([right_high, right_low, right_high], axis=side),
        (((1,), (side,)), ((), ())),
        preferred_element_type=jnp.float32,
    )


def add_diagonal(matrix, block):
    width = block.shape[0]
    count = matrix.shape[0] // width
    return jnp.concatenate(
        [
            jnp.concatenate(
                [
                    matrix[i * width : (i + 1) * width, j * width : (j + 1) * width] + (block if i == j else 0.0)
                    for j in range(count)
                ],
                axis=1,
            )
            for i in range(count)
        ],
        axis=0,
    )


def step_kernel(groups, place_ref, *refs):
    count = groups * PAIR
    shares = refs[: PAIR * count]
    upper_ref, lower_ref, new_upper_ref, new_lower_ref = refs[PAIR * count : PAIR * count + 4]
    rest_high, rest_low, low_high, low_low = refs[PAIR * count + 4 :]
    order, width = upper_ref.shape
    on_upper = place_ref[0] == 0
    square_shape = (width, width)
    unit = jnp.where(
        lax.broadcasted_iota(jnp.int32, square_shape, 0) == lax.broadcasted_iota(jnp.int32, square_shape, 1), 1.0, 0.0
    )
    total = jnp.zeros((8, width), jnp.float32)
    for step in range(groups):
        for side in range(PAIR):
            group = lax.rem(place_ref[1] + step, groups)
            column = group * PAIR + lax.rem(place_ref[2] + side, PAIR)
            same_ref = shares[step * PAIR + side]
            other_ref = shares[count + step * PAIR + side]
            same, other = same_ref[...], other_ref[...]
            head = jnp.where(on_upper, same, other)
            total = total + jnp.sum((head * head).reshape(-1, 8, width), axis=0)
            rest_high[column], rest_low[column] = halves(head)
            near = pl.ds(pl.multiple_of(column * width, width), width)
            diagonal = jnp.where(on_upper, same_ref[near, :], other_ref[near, :]) - LEAD * unit
            rest_high[column, near, :], rest_low[column, near, :] = halves(diagonal)
            low_high[column], low_low[column] = halves(jnp.where(on_upper, other, same))
    scale = lax.rsqrt(jnp.full((1, 1), jnp.sum(total)) / order + 1e-06)
    shift = 1.0 - LEAD * scale

    def joined(ref):
        return jnp.concatenate([ref[column] for column in range(count)], axis=1)

    rest = (joined(rest_high), joined(rest_low))
    low = (joined(low_high), joined(low_low))
    square = (scale * scale) * product(rest, rest) - (2.0 * shift * scale) * whole(rest)
    square = halves(add_diagonal(square, shift * shift * unit))
    middle = (1.0 + shift) * whole(low) - scale * product(low, rest)
    reflect = halves((middle + product(halves(middle), square)) * scale)
    upper = upper_ref[...].T
    lower = lower_ref[...].T
    gram = halves(product(reflect, reflect, 1))
    bent = product(halves(upper), reflect, 1)
    pulled = product(halves(jnp.concatenate([lower, bent], axis=0)), gram)
    both = jnp.concatenate([bent - pulled[:width], pulled[:width] - pulled[width:]], axis=0)
    inner = 0.3125 * both + 0.0625 * product(halves(both), gram)
    inner = 0.375 * both + product(halves(inner), gram)
    inner = 0.5 * both + product(halves(inner), gram)
    new_upper_ref[...] = (upper - product(halves(lower - inner[:width]), reflect)).T
    new_lower_ref[...] = (lower - bent + inner[width:]).T


def step_call(place, shares, upper, lower, groups):
    order, width = upper.shape
    count = groups * PAIR
    in_vmem = pl.BlockSpec(memory_space=pltpu.VMEM)
    return pl.pallas_call(
        functools.partial(step_kernel, groups),
        out_shape=(jax.ShapeDtypeStruct(upper.shape, jnp.float32),) * 2,
        in_specs=[pl.BlockSpec(memory_space=pltpu.SMEM)] + [in_vmem] * (len(shares) + 2),
        out_specs=(in_vmem, in_vmem),
        scratch_shapes=[pltpu.VMEM((count, order, width), jnp.bfloat16)] * 4,
        compiler_params=pltpu.CompilerParams(vmem_limit_bytes=48 * 1024 * 1024),
    )(place, *shares, upper, lower)


def spread(share, rows, row):
    stride = 1
    while stride < rows:
        stride *= 2
    while stride > 1:
        stride //= 2
        pairs = [(first, first + stride) for first in range(0, rows - stride, 2 * stride)]
        sends = [(PAIR * a + x, PAIR * b + x) for a, b in pairs for x in range(PAIR)]
        received = lax.ppermute(share, "blk", sends)
        share = jnp.where(lax.rem(row, 2 * stride) == stride, received, share)
    return share


def exchange(share, rows, groups):
    size = groups * PAIR
    shares = []
    for flip in range(PAIR):
        for step in range(groups):
            sends = [
                (
                    (PAIR * row + (x ^ flip)) * size + (y + step) % groups * PAIR + core,
                    (PAIR * row + x) * size + y * PAIR + core,
                )
                for row in range(rows)
                for x in range(PAIR)
                for y in range(groups)
                for core in range(PAIR)
            ]
            mine = lax.ppermute(share, ("blk", "col"), sends) if flip or step else share
            swap = [(column, column ^ 1) for column in range(size)]
            shares += [mine, lax.ppermute(mine, "col", swap)]
    return shares


def shards(upper_row, lower_row):
    blocks, size = lax.axis_size("blk"), lax.axis_size("col")
    assert upper_row.shape[1] == 1 and blocks % PAIR == 0 and size % PAIR == 0
    rows, groups = blocks // PAIR, size // PAIR
    block, column = lax.axis_index("blk"), lax.axis_index("col")
    upper, lower = upper_row[:, 0, :], lower_row[:, 0, :]
    side = lax.rem(block, PAIR)
    swapped = lax.ppermute(upper, "blk", [(source, source ^ 1) for source in range(blocks)])
    ahead = [(source, source + PAIR) for source in range(0, blocks - PAIR, PAIR)]
    shifted = jnp.where(side == 1, swapped, lax.ppermute(swapped, "blk", ahead))
    share = spread(jnp.where(side == 0, upper, lower), rows, block // PAIR)
    shares = exchange(share, rows, groups)
    place = jnp.stack([side, column // PAIR, lax.rem(column, PAIR)]).astype(jnp.int32)
    new_upper, new_lower = step_call(place, shares, shifted, lower, groups)
    return new_upper[:, None, :], new_lower[:, None, :]


def solution(mesh):
    placement = P(None, "blk", "col")
    return jax.shard_map(
        shards,
        mesh=mesh,
        in_specs=(placement, placement),
        out_specs=(placement, placement),
        check_vma=False,
    )
```

```python
import functools

import jax
import jax.numpy as jnp
from jax import lax
from jax.experimental import pallas as pl
from jax.experimental.pallas import tpu as pltpu
from jax.sharding import PartitionSpec as P

PAIR = 2
LEAD = 4.0


def halves(value):
    high = value.astype(jnp.bfloat16)
    return high, (value - high.astype(jnp.float32)).astype(jnp.bfloat16)


def whole(parts):
    return parts[0].astype(jnp.float32) + parts[1].astype(jnp.float32)


def dot(left, right, side):
    return lax.dot_general(left, right, (((1,), (side,)), ((), ())), preferred_element_type=jnp.float32)


def product(left, right, side=0):
    (left_high, left_low), (right_high, right_low) = left, right
    return dot(
        jnp.concatenate([left_high, left_high, left_low], axis=1),
        jnp.concatenate([right_high, right_low, right_high], axis=side),
        side,
    )


def thin_product(left, right, side=0):
    (left_high, left_low), (right_high, right_low) = halves(left), right
    both = dot(jnp.concatenate([left_high, left_low], axis=0), right_high, side)
    return both[: left.shape[0]] + both[left.shape[0] :] + dot(left_high, right_low, side)


def inner_product(left, gram):
    inner = 0.3125 * left + 0.0625 * thin_product(left, gram)
    inner = 0.375 * left + thin_product(inner, gram)
    return 0.5 * left + thin_product(inner, gram)


def add_diagonal(matrix, block):
    width = block.shape[0]
    count = matrix.shape[0] // width
    return jnp.concatenate(
        [
            jnp.concatenate(
                [
                    matrix[i * width : (i + 1) * width, j * width : (j + 1) * width] + (block if i == j else 0.0)
                    for j in range(count)
                ],
                axis=1,
            )
            for i in range(count)
        ],
        axis=0,
    )


def step_kernel(groups, *refs):
    count = groups * PAIR
    block, here = lax.axis_index("blk"), lax.axis_index("col")
    shares = refs[: PAIR * count]
    upper_ref, lower_ref, new_upper_ref, new_lower_ref = refs[PAIR * count : PAIR * count + 4]
    rest_high, rest_low, low_high, low_low, made_upper, made_lower, sent = refs[PAIR * count + 4 :]
    order, width = upper_ref.shape
    on_upper = lax.rem(block, PAIR) == 0
    square_shape = (width, width)
    unit = jnp.where(
        lax.broadcasted_iota(jnp.int32, square_shape, 0) == lax.broadcasted_iota(jnp.int32, square_shape, 1), 1.0, 0.0
    )
    total = jnp.zeros((8, width), jnp.float32)
    for step in range(groups):
        for side in range(PAIR):
            group = lax.rem(here // PAIR + step, groups)
            column = group * PAIR + lax.rem(here + side, PAIR)
            same_ref = shares[step * PAIR + side]
            other_ref = shares[count + step * PAIR + side]
            same, other = same_ref[...], other_ref[...]
            head = jnp.where(on_upper, same, other)
            total = total + jnp.sum((head * head).reshape(-1, 8, width), axis=0)
            rest_high[column], rest_low[column] = halves(head)
            near = pl.ds(pl.multiple_of(column * width, width), width)
            diagonal = jnp.where(on_upper, same_ref[near, :], other_ref[near, :]) - LEAD * unit
            rest_high[column, near, :], rest_low[column, near, :] = halves(diagonal)
            low_high[column], low_low[column] = halves(jnp.where(on_upper, other, same))
    scale = lax.rsqrt(jnp.full((1, 1), jnp.sum(total)) / order + 1e-06)
    shift = 1.0 - LEAD * scale

    def joined(ref):
        return jnp.concatenate([ref[column] for column in range(count)], axis=1)

    rest = (joined(rest_high), joined(rest_low))
    low = (joined(low_high), joined(low_low))
    square = (scale * scale) * product(rest, rest) - (2.0 * shift * scale) * whole(rest)
    square = halves(add_diagonal(square, shift * shift * unit))
    middle = (1.0 + shift) * whole(low) - scale * product(low, rest)
    reflect = halves((middle + product(halves(middle), square)) * scale)
    upper = upper_ref[...].T
    lower = lower_ref[...].T
    gram = halves(product(reflect, reflect, 1))
    bent = thin_product(upper, reflect, 1)
    pulled = thin_product(lower, gram)
    inner_upper = inner_product(bent - pulled, gram)
    inner_lower = inner_product(pulled - thin_product(bent, gram), gram)
    made_lower[...] = (lower - bent + inner_lower).T
    lower_copy = pltpu.make_async_copy(made_lower, new_lower_ref, sent.at[0])
    lower_copy.start()
    made_upper[...] = (upper - thin_product(lower - inner_upper, reflect)).T
    upper_copy = pltpu.make_async_copy(made_upper, new_upper_ref, sent.at[1])
    upper_copy.start()
    lower_copy.wait()
    upper_copy.wait()


def step_call(shares, upper, lower, groups):
    order, width = upper.shape
    count = groups * PAIR
    in_vmem = pl.BlockSpec(memory_space=pltpu.VMEM)
    return pl.pallas_call(
        functools.partial(step_kernel, groups),
        out_shape=(jax.ShapeDtypeStruct(upper.shape, jnp.float32),) * 2,
        in_specs=[in_vmem] * (len(shares) + 2),
        out_specs=(pl.BlockSpec(memory_space=pl.ANY),) * 2,
        scratch_shapes=[pltpu.VMEM((count, order, width), jnp.bfloat16)] * 4
        + [pltpu.VMEM((order, width), jnp.float32)] * 2
        + [pltpu.SemaphoreType.DMA((2,))],
        compiler_params=pltpu.CompilerParams(vmem_limit_bytes=48 * 1024 * 1024),
    )(*shares, upper, lower)


def spread(upper, lower, rows, row, flip):
    stride = 1
    while stride < rows:
        stride *= 2
    share = lax.optimization_barrier(jnp.where(flip == 0, upper, lower))
    while stride > 1:
        stride //= 2
        pairs = [(first, first + stride) for first in range(0, rows - stride, 2 * stride)]
        sends = [[(PAIR * a + x, PAIR * b + x) for a, b in pairs] for x in range(PAIR)]
        if 2 * stride >= rows:
            received = jnp.where(
                flip == 0, lax.ppermute(upper, "blk", sends[0]), lax.ppermute(lower, "blk", sends[1])
            )
        else:
            received = lax.ppermute(share, "blk", sends[0] + sends[1])
        share = jnp.where(lax.rem(row, 2 * stride) == stride, received, share)
    return share


def exchange(share, rows, groups):
    size = groups * PAIR
    shares = []
    for flip in range(PAIR):
        for step in range(groups):
            sends = [
                (
                    (PAIR * row + (x ^ flip)) * size + (y + step) % groups * PAIR + core,
                    (PAIR * row + x) * size + y * PAIR + core,
                )
                for row in range(rows)
                for x in range(PAIR)
                for y in range(groups)
                for core in range(PAIR)
            ]
            mine = lax.ppermute(share, ("blk", "col"), sends) if flip or step else share
            swap = [(column, column ^ 1) for column in range(size)]
            shares += [mine, lax.ppermute(mine, "col", swap)]
    return shares


def shards(upper_row, lower_row):
    blocks, size = lax.axis_size("blk"), lax.axis_size("col")
    assert upper_row.shape[1] == 1 and blocks % PAIR == 0 and size % PAIR == 0
    rows, groups = blocks // PAIR, size // PAIR
    block = lax.axis_index("blk")
    upper, lower = upper_row[:, 0, :], lower_row[:, 0, :]
    side = lax.rem(block, PAIR)
    swapped = lax.ppermute(upper, "blk", [(source, source ^ 1) for source in range(blocks)])
    ahead = [(source, source + PAIR) for source in range(0, blocks - PAIR, PAIR)]
    shifted = jnp.where(side == 1, swapped, lax.ppermute(swapped, "blk", ahead))
    share = spread(upper, lower, rows, block // PAIR, side)
    shares = exchange(share, rows, groups)
    new_upper, new_lower = step_call(shares, shifted, lower, groups)
    return new_upper[:, None, :], new_lower[:, None, :]


def solution(mesh):
    placement = P(None, "blk", "col")
    return jax.shard_map(
        shards,
        mesh=mesh,
        in_specs=(placement, placement),
        out_specs=(placement, placement),
        check_vma=False,
    )
```

```python
import functools

import jax
import jax.numpy as jnp
from jax import lax
from jax.experimental import pallas as pl
from jax.experimental.pallas import tpu as pltpu
from jax.sharding import PartitionSpec as P

PAIR = 2
LEAD = 4.0


def halves(value):
    high = value.astype(jnp.bfloat16)
    return high, (value - high.astype(jnp.float32)).astype(jnp.bfloat16)


def whole(parts):
    return parts[0].astype(jnp.float32) + parts[1].astype(jnp.float32)


def dot(left, right, side):
    return lax.dot_general(left, right, (((1,), (side,)), ((), ())), preferred_element_type=jnp.float32)


def product(left, right, side=0):
    (left_high, left_low), (right_high, right_low) = left, right
    return dot(
        jnp.concatenate([left_high, left_high, left_low], axis=1),
        jnp.concatenate([right_high, right_low, right_high], axis=side),
        side,
    )


def thin_product(left, right, side=0):
    (left_high, left_low), (right_high, right_low) = halves(left), right
    both = dot(jnp.concatenate([left_high, left_low], axis=0), right_high, side)
    return both[: left.shape[0]] + both[left.shape[0] :] + dot(left_high, right_low, side)


def add_diagonal(matrix, block):
    width = block.shape[0]
    count = matrix.shape[0] // width
    return jnp.concatenate(
        [
            jnp.concatenate(
                [
                    matrix[i * width : (i + 1) * width, j * width : (j + 1) * width] + (block if i == j else 0.0)
                    for j in range(count)
                ],
                axis=1,
            )
            for i in range(count)
        ],
        axis=0,
    )


def step_kernel(groups, *refs):
    count = groups * PAIR
    shares = refs[: PAIR * count]
    upper_ref, lower_ref, new_upper_ref, new_lower_ref = refs[PAIR * count : PAIR * count + 4]
    rest_high, rest_low, low_high, low_low, made_upper, made_lower, sent = refs[PAIR * count + 4 :]
    order, width = upper_ref.shape
    block, here = lax.axis_index("blk"), lax.axis_index("col")
    on_upper = lax.rem(block, PAIR) == 0
    square_shape = (width, width)
    unit = jnp.where(
        lax.broadcasted_iota(jnp.int32, square_shape, 0) == lax.broadcasted_iota(jnp.int32, square_shape, 1), 1.0, 0.0
    )
    rows = []
    for step in range(groups):
        for side in range(PAIR):
            column = lax.rem(here // PAIR + step, groups) * PAIR + lax.rem(here + side, PAIR)
            rows.append(pl.ds(pl.multiple_of(column * width, width), width))
    total = jnp.zeros((8, width), jnp.float32)
    for i in range(count):
        columns = slice(i * width, (i + 1) * width)
        for j in range(count):
            head = jnp.where(on_upper, shares[i][rows[j], :], shares[count + i][rows[j], :])
            total = total + jnp.sum((head * head).reshape(-1, 8, width), axis=0)
            to = slice(j * width, (j + 1) * width)
            rest_high[to, columns], rest_low[to, columns] = halves(head - LEAD * unit if i == j else head)
        low_high[:, columns], low_low[:, columns] = halves(jnp.where(on_upper, shares[count + i][...], shares[i][...]))
    scale = lax.rsqrt(jnp.full((1, 1), jnp.sum(total)) / order + 1e-06)
    shift = 1.0 - LEAD * scale
    rest = (rest_high[...], rest_low[...])
    low = (low_high[...], low_low[...])
    square = (scale * scale) * product(rest, rest) - (2.0 * shift * scale) * whole(rest)
    square = halves(add_diagonal(square, shift * shift * unit))
    middle = (1.0 + shift) * whole(low) - scale * product(low, rest)
    reflect = halves((middle + product(halves(middle), square)) * scale)
    upper = jnp.concatenate([upper_ref[part, :].T for part in rows], axis=1)
    lower = lower_ref[...].T
    gram = halves(product(reflect, reflect, 1))
    bent = thin_product(upper, reflect, 1)
    pulled = thin_product(lower, gram)
    bases = [bent - pulled, pulled - thin_product(bent, gram)]
    inners = [0.3125 * base + 0.0625 * thin_product(base, gram) for base in bases]
    inners = [0.375 * base + thin_product(inner, gram) for base, inner in zip(bases, inners)]
    inner_upper, inner_lower = [0.5 * base + thin_product(inner, gram) for base, inner in zip(bases, inners)]
    made_lower[...] = (lower - bent + inner_lower).T
    lower_copy = pltpu.make_async_copy(made_lower, new_lower_ref, sent.at[0])
    lower_copy.start()
    upper = upper - thin_product(lower - inner_upper, reflect)
    for i, part in enumerate(rows):
        made_upper[part, :] = upper[:, i * width : (i + 1) * width].T
    upper_copy = pltpu.make_async_copy(made_upper, new_upper_ref, sent.at[1])
    upper_copy.start()
    lower_copy.wait()
    upper_copy.wait()


def step_call(shares, upper, lower, groups):
    order, width = upper.shape
    count = groups * PAIR
    in_vmem = pl.BlockSpec(memory_space=pltpu.VMEM)
    return pl.pallas_call(
        functools.partial(step_kernel, groups),
        out_shape=(jax.ShapeDtypeStruct(upper.shape, jnp.float32),) * 2,
        in_specs=[in_vmem] * (len(shares) + 2),
        out_specs=(pl.BlockSpec(memory_space=pl.ANY),) * 2,
        scratch_shapes=[pltpu.VMEM((order, order), jnp.bfloat16)] * 4
        + [pltpu.VMEM((order, width), jnp.float32)] * 2
        + [pltpu.SemaphoreType.DMA((2,))],
        compiler_params=pltpu.CompilerParams(vmem_limit_bytes=48 * 1024 * 1024),
    )(*shares, upper, lower)


def spread(upper, lower, rows, row, flip):
    stride = 1
    while stride < rows:
        stride *= 2
    share = lax.optimization_barrier(jnp.where(flip == 0, upper, lower))
    while stride > 1:
        stride //= 2
        pairs = [(first, first + stride) for first in range(0, rows - stride, 2 * stride)]
        sends = [[(PAIR * a + x, PAIR * b + x) for a, b in pairs] for x in range(PAIR)]
        if 2 * stride >= rows:
            received = jnp.where(
                flip == 0, lax.ppermute(upper, "blk", sends[0]), lax.ppermute(lower, "blk", sends[1])
            )
        else:
            received = lax.ppermute(share, "blk", sends[0] + sends[1])
        share = jnp.where(lax.rem(row, 2 * stride) == stride, received, share)
    return share


def exchange(share, rows, groups):
    size = groups * PAIR
    shares = []
    for flip in range(PAIR):
        for step in range(groups):
            sends = [
                (
                    (PAIR * row + (x ^ flip)) * size + (y + step) % groups * PAIR + core,
                    (PAIR * row + x) * size + y * PAIR + core,
                )
                for row in range(rows)
                for x in range(PAIR)
                for y in range(groups)
                for core in range(PAIR)
            ]
            mine = lax.ppermute(share, ("blk", "col"), sends) if flip or step else share
            swap = [(column, column ^ 1) for column in range(size)]
            shares += [mine, lax.ppermute(mine, "col", swap)]
    return shares


def shards(upper_row, lower_row):
    blocks, size = lax.axis_size("blk"), lax.axis_size("col")
    assert upper_row.shape[1] == 1 and blocks % PAIR == 0 and size % PAIR == 0
    rows, groups = blocks // PAIR, size // PAIR
    block = lax.axis_index("blk")
    upper, lower = upper_row[:, 0, :], lower_row[:, 0, :]
    side = lax.rem(block, PAIR)
    swapped = lax.ppermute(upper, "blk", [(source, source ^ 1) for source in range(blocks)])
    ahead = [(source, source + PAIR) for source in range(0, blocks - PAIR, PAIR)]
    shifted = jnp.where(side == 1, swapped, lax.ppermute(swapped, "blk", ahead))
    share = spread(upper, lower, rows, block // PAIR, side)
    shares = exchange(share, rows, groups)
    new_upper, new_lower = step_call(shares, shifted, lower, groups)
    return new_upper[:, None, :], new_lower[:, None, :]


def solution(mesh):
    placement = P(None, "blk", "col")
    return jax.shard_map(
        shards,
        mesh=mesh,
        in_specs=(placement, placement),
        out_specs=(placement, placement),
        check_vma=False,
    )
```

```python
import functools

import jax
import jax.numpy as jnp
from jax import lax
from jax.experimental import pallas as pl
from jax.experimental.pallas import tpu as pltpu
from jax.sharding import PartitionSpec as P

PAIR = 2
QUARTET = 4
LEAD = 4.0


def halves(value):
    high = value.astype(jnp.bfloat16)
    return high, (value - high.astype(jnp.float32)).astype(jnp.bfloat16)


def dot(left, right, side):
    return lax.dot_general(left, right, (((1,), (side,)), ((), ())), preferred_element_type=jnp.float32)


def product(left, right, side=0):
    (left_high, left_low), (right_high, right_low) = left, right
    return dot(
        jnp.concatenate([left_high, left_high, left_low], axis=1),
        jnp.concatenate([right_high, right_low, right_high], axis=side),
        side,
    )


def thin_product(left, right, side=0):
    (left_high, left_low), (right_high, right_low) = halves(left), right
    both = dot(jnp.concatenate([left_high, left_low], axis=0), right_high, side)
    return both[: left.shape[0]] + both[left.shape[0] :] + dot(left_high, right_low, side)


def step_kernel(groups, *refs):
    count = groups * PAIR
    shares = refs[: PAIR * count]
    upper_ref, lower_ref, new_upper_ref, new_lower_ref = refs[PAIR * count : PAIR * count + 4]
    rest_high, rest_low, made_upper, made_lower, sent = refs[PAIR * count + 4 :]
    order, width = upper_ref.shape
    block, here = lax.axis_index("blk"), lax.axis_index("col")
    on_upper = lax.rem(block, PAIR) == 0
    square_shape = (width, width)
    unit = jnp.where(
        lax.broadcasted_iota(jnp.int32, square_shape, 0) == lax.broadcasted_iota(jnp.int32, square_shape, 1), 1.0, 0.0
    )
    rows = []
    for step in range(groups):
        for side in range(PAIR):
            column = lax.rem(here // PAIR + step, groups) * PAIR + lax.rem(here + side, PAIR)
            rows.append(pl.ds(pl.multiple_of(column * width, width), width))
    total = jnp.zeros((8, width), jnp.float32)
    for i in range(count):
        columns = slice(i * width, (i + 1) * width)
        for j in range(count):
            head = jnp.where(on_upper, shares[i][rows[j], :], shares[count + i][rows[j], :])
            total = total + jnp.sum((head * head).reshape(-1, 8, width), axis=0)
            to = slice(j * width, (j + 1) * width)
            rest_high[to, columns], rest_low[to, columns] = halves(head - LEAD * unit if i == j else head)
    scale = lax.rsqrt(jnp.full((1, 1), jnp.sum(total)) / order + 1e-06)
    shift = 1.0 - LEAD * scale
    rest = (rest_high[...], rest_low[...])
    strips = []
    for first in range(0, order, order // 2):
        strip = slice(first, first + order // 2)
        parts = [jnp.where(on_upper, shares[count + i][strip, :], shares[i][strip, :]) for i in range(count)]
        strips.append(jnp.concatenate(parts, axis=1))
    powers, sums = strips, strips
    for _ in range(3):
        powers = [shift * power - scale * thin_product(power, rest) for power in powers]
        sums = [total + power for total, power in zip(sums, powers)]
    reflects = [halves(total * scale) for total in sums]
    reflect = tuple(jnp.concatenate(parts, axis=0) for parts in zip(*reflects))
    upper = jnp.concatenate([upper_ref[part, :].T for part in rows], axis=1)
    lower = lower_ref[...].T
    gram = halves(product(reflect, reflect, 1))
    bent = thin_product(upper, reflect, 1)
    pulled = thin_product(lower, gram)
    bases = [bent - pulled, pulled - thin_product(bent, gram)]
    inners = [0.3125 * base + 0.0625 * thin_product(base, gram) for base in bases]
    inners = [0.375 * base + thin_product(inner, gram) for base, inner in zip(bases, inners)]
    inner_upper, inner_lower = [0.5 * base + thin_product(inner, gram) for base, inner in zip(bases, inners)]
    made_lower[...] = (lower - bent + inner_lower).T
    lower_copy = pltpu.make_async_copy(made_lower, new_lower_ref, sent.at[0])
    lower_copy.start()
    upper = upper - thin_product(lower - inner_upper, reflect)
    for i, part in enumerate(rows):
        made_upper[part, :] = upper[:, i * width : (i + 1) * width].T
    upper_copy = pltpu.make_async_copy(made_upper, new_upper_ref, sent.at[1])
    upper_copy.start()
    lower_copy.wait()
    upper_copy.wait()


def step_call(shares, upper, lower, groups):
    order, width = upper.shape
    count = groups * PAIR
    in_vmem = pl.BlockSpec(memory_space=pltpu.VMEM)
    return pl.pallas_call(
        functools.partial(step_kernel, groups),
        out_shape=(jax.ShapeDtypeStruct(upper.shape, jnp.float32),) * 2,
        in_specs=[in_vmem] * (len(shares) + 2),
        out_specs=(pl.BlockSpec(memory_space=pl.ANY),) * 2,
        scratch_shapes=[pltpu.VMEM((order, order), jnp.bfloat16)] * 2
        + [pltpu.VMEM((order, width), jnp.float32)] * 2
        + [pltpu.SemaphoreType.DMA((2,))],
        compiler_params=pltpu.CompilerParams(vmem_limit_bytes=48 * 1024 * 1024),
    )(*shares, upper, lower)


def spread(share, moved, rows, row):
    def send(value, moves):
        pairs = []
        for first in range(0, rows, QUARTET):
            pairs += [(PAIR * (first + a) + x, PAIR * (first + b) + x) for a, b in moves for x in range(PAIR)]
        return lax.ppermute(value, "blk", pairs)

    assert rows % QUARTET == 0
    stride = QUARTET
    while stride < rows:
        stride *= 2
    while stride > QUARTET:
        stride //= 2
        heads = range(0, rows - stride, 2 * stride)
        pairs = [(PAIR * a + x, PAIR * (a + stride) + x) for a in heads for x in range(PAIR)]
        received = lax.ppermute(share, "blk", pairs)
        share = jnp.where(lax.rem(row, 2 * stride) == stride, received, share)
    place = lax.rem(row, QUARTET)
    cut = share.shape[0] // 2 - 8
    top, bottom = share[:cut], share[cut:]
    top_one = send(top, [(0, 1)])
    bottom_two = send(bottom, [(0, 2)])
    bottom_one = send(bottom, [(0, 1)])
    top_one, bottom_two = lax.optimization_barrier((top_one, bottom_two))
    top_three = send(top_one, [(1, 3)])
    top_two = send(top_one, [(1, 2)])
    bottom_three = send(bottom_two, [(2, 3)])
    bottom_one, moved = lax.optimization_barrier((bottom_one, moved))
    top = jnp.where(place == 0, top, jnp.where(place == 1, top_one, jnp.where(place == 2, top_two, top_three)))
    bottom = jnp.where(
        place == 0, bottom, jnp.where(place == 1, bottom_one, jnp.where(place == 2, bottom_two, bottom_three))
    )
    return jnp.concatenate([top, bottom], axis=0), moved


def exchange(share, rows, groups):
    size = groups * PAIR
    shares = []
    for flip in range(PAIR):
        for step in range(groups):
            sends = [
                (
                    (PAIR * row + (x ^ flip)) * size + (y + step) % groups * PAIR + core,
                    (PAIR * row + x) * size + y * PAIR + core,
                )
                for row in range(rows)
                for x in range(PAIR)
                for y in range(groups)
                for core in range(PAIR)
            ]
            mine = lax.ppermute(share, ("blk", "col"), sends) if flip or step else share
            swap = [(column, column ^ 1) for column in range(size)]
            shares += [mine, lax.ppermute(mine, "col", swap)]
    return shares


def shards(upper_row, lower_row):
    blocks, size = lax.axis_size("blk"), lax.axis_size("col")
    assert upper_row.shape[1] == 1 and blocks % PAIR == 0 and size % PAIR == 0
    rows, groups = blocks // PAIR, size // PAIR
    block = lax.axis_index("blk")
    upper, lower = upper_row[:, 0, :], lower_row[:, 0, :]
    side = lax.rem(block, PAIR)
    swapped = lax.ppermute(upper, "blk", [(source, source ^ 1) for source in range(blocks)])
    share = jnp.where(side == 0, upper, lower)
    share, swapped = spread(share, swapped, rows, block // PAIR)
    forward = [(source, (source + PAIR) % blocks) for source in range(blocks)]
    onward = lax.ppermute(swapped, "blk", forward)
    shifted = jnp.where(side == 1, swapped, jnp.where(block == 0, 0.0, onward))
    shares = exchange(share, rows, groups)
    new_upper, new_lower = step_call(shares, shifted, lower, groups)
    return new_upper[:, None, :], new_lower[:, None, :]


def solution(mesh):
    placement = P(None, "blk", "col")
    return jax.shard_map(
        shards,
        mesh=mesh,
        in_specs=(placement, placement),
        out_specs=(placement, placement),
        check_vma=False,
    )
```

```python
import functools

import jax
import jax.numpy as jnp
from jax import lax
from jax.experimental import pallas as pl
from jax.experimental.pallas import tpu as pltpu
from jax.sharding import PartitionSpec as P

PAIR = 2
QUARTET = 4
LEAD = 4.0


def halves(value):
    high = value.astype(jnp.bfloat16)
    return high, (value - high.astype(jnp.float32)).astype(jnp.bfloat16)


def dot(left, right, side):
    return lax.dot_general(left, right, (((1,), (side,)), ((), ())), preferred_element_type=jnp.float32)


def product(left, right, side=0):
    (left_high, left_low), (right_high, right_low) = left, right
    return dot(
        jnp.concatenate([left_high, left_high, left_low], axis=1),
        jnp.concatenate([right_high, right_low, right_high], axis=side),
        side,
    )


def thin_product(left, right, side=0):
    (left_high, left_low), (right_high, right_low) = halves(left), right
    both = dot(jnp.concatenate([left_high, left_low], axis=0), right_high, side)
    return both[: left.shape[0]] + both[left.shape[0] :] + dot(left_high, right_low, side)


def step_kernel(groups, *refs):
    count = groups * PAIR
    shares = refs[: PAIR * count]
    upper_ref, lower_ref, new_upper_ref, new_lower_ref = refs[PAIR * count : PAIR * count + 4]
    rest_high, rest_low, made_upper, made_lower, sent = refs[PAIR * count + 4 :]
    order, width = upper_ref.shape
    block, here = lax.axis_index("blk"), lax.axis_index("col")
    on_upper = lax.rem(block, PAIR) == 0
    square_shape = (width, width)
    unit = jnp.where(
        lax.broadcasted_iota(jnp.int32, square_shape, 0) == lax.broadcasted_iota(jnp.int32, square_shape, 1), 1.0, 0.0
    )
    rows = []
    for step in range(groups):
        for side in range(PAIR):
            column = lax.rem(here // PAIR + step, groups) * PAIR + lax.rem(here + side, PAIR)
            rows.append(pl.ds(pl.multiple_of(column * width, width), width))
    total = jnp.zeros((8, width), jnp.float32)
    for i in range(count):
        columns = slice(i * width, (i + 1) * width)
        for j in range(count):
            head = jnp.where(on_upper, shares[i][rows[j], :], shares[count + i][rows[j], :])
            total = total + jnp.sum((head * head).reshape(-1, 8, width), axis=0)
            to = slice(j * width, (j + 1) * width)
            rest_high[to, columns], rest_low[to, columns] = halves(head - LEAD * unit if i == j else head)
    scale = lax.rsqrt(jnp.full((1, 1), jnp.sum(total)) / order + 1e-06)
    shift = 1.0 - LEAD * scale
    rest = (rest_high[...], rest_low[...])
    strips = []
    for first in range(0, order, order // 2):
        strip = slice(first, first + order // 2)
        parts = [jnp.where(on_upper, shares[count + i][strip, :], shares[i][strip, :]) for i in range(count)]
        strips.append(jnp.concatenate(parts, axis=1))
    powers, sums = strips, strips
    for _ in range(3):
        powers = [shift * power - scale * thin_product(power, rest) for power in powers]
        sums = [total + power for total, power in zip(sums, powers)]
    reflects = [halves(total * scale) for total in sums]
    reflect = tuple(jnp.concatenate(parts, axis=0) for parts in zip(*reflects))
    upper = jnp.concatenate([upper_ref[part, :].T for part in rows], axis=1)
    lower = lower_ref[...].T
    gram = halves(product(reflect, reflect, 1))
    bent = thin_product(upper, reflect, 1)
    pulled = thin_product(lower, gram)
    bases = [bent - pulled, pulled - thin_product(bent, gram)]
    inners = [0.3125 * base + 0.0625 * thin_product(base, gram) for base in bases]
    inners = [0.375 * base + thin_product(inner, gram) for base, inner in zip(bases, inners)]
    inner_upper, inner_lower = [0.5 * base + thin_product(inner, gram) for base, inner in zip(bases, inners)]
    made_lower[...] = (lower - bent + inner_lower).T
    lower_copy = pltpu.make_async_copy(made_lower, new_lower_ref, sent.at[0])
    lower_copy.start()
    upper = upper - thin_product(lower - inner_upper, reflect)
    for i, part in enumerate(rows):
        made_upper[part, :] = upper[:, i * width : (i + 1) * width].T
    upper_copy = pltpu.make_async_copy(made_upper, new_upper_ref, sent.at[1])
    upper_copy.start()
    lower_copy.wait()
    upper_copy.wait()


def step_call(shares, upper, lower, groups):
    order, width = upper.shape
    count = groups * PAIR
    in_vmem = pl.BlockSpec(memory_space=pltpu.VMEM)
    return pl.pallas_call(
        functools.partial(step_kernel, groups),
        out_shape=(jax.ShapeDtypeStruct(upper.shape, jnp.float32),) * 2,
        in_specs=[in_vmem] * (len(shares) + 2),
        out_specs=(pl.BlockSpec(memory_space=pl.ANY),) * 2,
        scratch_shapes=[pltpu.VMEM((order, order), jnp.bfloat16)] * 2
        + [pltpu.VMEM((order, width), jnp.float32)] * 2
        + [pltpu.SemaphoreType.DMA((2,))],
        compiler_params=pltpu.CompilerParams(vmem_limit_bytes=48 * 1024 * 1024),
    )(*shares, upper, lower)


def spread(share, moved, rows, row):
    def send(value, moves):
        pairs = []
        for first in range(0, rows, QUARTET):
            pairs += [(PAIR * (first + a) + x, PAIR * (first + b) + x) for a, b in moves for x in range(PAIR)]
        return lax.ppermute(value, "blk", pairs)

    assert rows % QUARTET == 0
    stride = QUARTET
    while stride < rows:
        stride *= 2
    while stride > QUARTET:
        stride //= 2
        heads = range(0, rows - stride, 2 * stride)
        pairs = [(PAIR * a + x, PAIR * (a + stride) + x) for a in heads for x in range(PAIR)]
        received = lax.ppermute(share, "blk", pairs)
        share = jnp.where(lax.rem(row, 2 * stride) == stride, received, share)
    place = lax.rem(row, QUARTET)
    top, bottom = jnp.split(share, 2, axis=0)
    top_one = send(top, [(0, 1), (1, 0), (2, 3), (3, 2)])
    bottom_two = send(bottom, [(0, 2)])
    holds = jnp.where(place == 1, top_one, jnp.where(place == 2, bottom_two, bottom))
    top_three = send(top_one, [(1, 3)])
    passed = send(holds, [(0, 1), (1, 2), (2, 3), (3, 0)])
    top_three, moved = lax.optimization_barrier((top_three, moved))
    top = jnp.where(place == 0, top, jnp.where(place == 1, top_one, jnp.where(place == 2, passed, top_three)))
    bottom = jnp.where(place == 0, bottom, jnp.where(place == 2, bottom_two, passed))
    return jnp.concatenate([top, bottom], axis=0), moved


def exchange(share, rows, groups):
    size = groups * PAIR
    shares = []
    for flip in range(PAIR):
        for step in range(groups):
            sends = [
                (
                    (PAIR * row + (x ^ flip)) * size + (y + step) % groups * PAIR + core,
                    (PAIR * row + x) * size + y * PAIR + core,
                )
                for row in range(rows)
                for x in range(PAIR)
                for y in range(groups)
                for core in range(PAIR)
            ]
            mine = lax.ppermute(share, ("blk", "col"), sends) if flip or step else share
            swap = [(column, column ^ 1) for column in range(size)]
            shares += [mine, lax.ppermute(mine, "col", swap)]
    return shares


def shards(upper_row, lower_row):
    blocks, size = lax.axis_size("blk"), lax.axis_size("col")
    assert upper_row.shape[1] == 1 and blocks % PAIR == 0 and size % PAIR == 0
    rows, groups = blocks // PAIR, size // PAIR
    block = lax.axis_index("blk")
    upper, lower = upper_row[:, 0, :], lower_row[:, 0, :]
    side = lax.rem(block, PAIR)
    swapped = lax.ppermute(upper, "blk", [(source, source ^ 1) for source in range(blocks)])
    share = jnp.where(side == 0, upper, lower)
    share, swapped = spread(share, swapped, rows, block // PAIR)
    forward = [(source, (source + PAIR) % blocks) for source in range(blocks)]
    onward = lax.ppermute(swapped, "blk", forward)
    shifted = jnp.where(side == 1, swapped, jnp.where(block == 0, 0.0, onward))
    shares = exchange(share, rows, groups)
    new_upper, new_lower = step_call(shares, shifted, lower, groups)
    return new_upper[:, None, :], new_lower[:, None, :]


def solution(mesh):
    placement = P(None, "blk", "col")
    return jax.shard_map(
        shards,
        mesh=mesh,
        in_specs=(placement, placement),
        out_specs=(placement, placement),
        check_vma=False,
    )
```

```python
import functools

import jax
import jax.numpy as jnp
from jax import lax
from jax.experimental import pallas as pl
from jax.experimental.pallas import tpu as pltpu
from jax.sharding import PartitionSpec as P

PAIR = 2
QUARTET = 4
LEAD = 4.0


def halves(value):
    high = value.astype(jnp.bfloat16)
    return high, (value - high.astype(jnp.float32)).astype(jnp.bfloat16)


def dot(left, right, side):
    return lax.dot_general(left, right, (((1,), (side,)), ((), ())), preferred_element_type=jnp.float32)


def product(left, right, side=0):
    (left_high, left_low), (right_high, right_low) = left, right
    return dot(
        jnp.concatenate([left_high, left_high, left_low], axis=1),
        jnp.concatenate([right_high, right_low, right_high], axis=side),
        side,
    )


def thin_product(left, right, side=0):
    (left_high, left_low), (right_high, right_low) = halves(left), right
    both = dot(jnp.concatenate([left_high, left_low], axis=0), right_high, side)
    return both[: left.shape[0]] + both[left.shape[0] :] + dot(left_high, right_low, side)


def step_kernel(groups, *refs):
    count = groups * PAIR
    shares = refs[: PAIR * count]
    upper_ref, lower_ref, new_upper_ref, new_lower_ref = refs[PAIR * count : PAIR * count + 4]
    rest_high, rest_low, made_upper, made_lower, sent = refs[PAIR * count + 4 :]
    order, width = upper_ref.shape
    block, here = lax.axis_index("blk"), lax.axis_index("col")
    on_upper = lax.rem(block, PAIR) == 0
    square_shape = (width, width)
    unit = jnp.where(
        lax.broadcasted_iota(jnp.int32, square_shape, 0) == lax.broadcasted_iota(jnp.int32, square_shape, 1), 1.0, 0.0
    )
    rows = []
    for step in range(groups):
        for side in range(PAIR):
            column = lax.rem(here // PAIR + step, groups) * PAIR + lax.rem(here + side, PAIR)
            rows.append(pl.ds(pl.multiple_of(column * width, width), width))
    total = jnp.zeros((8, width), jnp.float32)
    for i in range(count):
        columns = slice(i * width, (i + 1) * width)
        for j in range(count):
            head = jnp.where(on_upper, shares[i][rows[j], :], shares[count + i][rows[j], :])
            total = total + jnp.sum((head * head).reshape(-1, 8, width), axis=0)
            to = slice(j * width, (j + 1) * width)
            rest_high[to, columns], rest_low[to, columns] = halves(head - LEAD * unit if i == j else head)
    scale = lax.rsqrt(jnp.full((1, 1), jnp.sum(total)) / order + 1e-06)
    shift = 1.0 - LEAD * scale
    rest = (rest_high[...], rest_low[...])
    strips = []
    for first in range(0, order, order // 2):
        strip = slice(first, first + order // 2)
        parts = [jnp.where(on_upper, shares[count + i][strip, :], shares[i][strip, :]) for i in range(count)]
        strips.append(jnp.concatenate(parts, axis=1))
    powers, sums = strips, strips
    for _ in range(3):
        powers = [shift * power - scale * thin_product(power, rest) for power in powers]
        sums = [total + power for total, power in zip(sums, powers)]
    reflects = [halves(total * scale) for total in sums]
    reflect = tuple(jnp.concatenate(parts, axis=0) for parts in zip(*reflects))
    upper = jnp.concatenate([upper_ref[part, :].T for part in rows], axis=1)
    lower = lower_ref[...].T
    gram = halves(product(reflect, reflect, 1))
    bent = thin_product(upper, reflect, 1)
    pulled = thin_product(lower, gram)
    bases = [bent - pulled, pulled - thin_product(bent, gram)]
    inners = [0.3125 * base + 0.0625 * thin_product(base, gram) for base in bases]
    inners = [0.375 * base + thin_product(inner, gram) for base, inner in zip(bases, inners)]
    inner_upper, inner_lower = [0.5 * base + thin_product(inner, gram) for base, inner in zip(bases, inners)]
    made_lower[...] = (lower - bent + inner_lower).T
    lower_copy = pltpu.make_async_copy(made_lower, new_lower_ref, sent.at[0])
    lower_copy.start()
    upper = upper - thin_product(lower - inner_upper, reflect)
    for i, part in enumerate(rows):
        made_upper[part, :] = upper[:, i * width : (i + 1) * width].T
    upper_copy = pltpu.make_async_copy(made_upper, new_upper_ref, sent.at[1])
    upper_copy.start()
    lower_copy.wait()
    upper_copy.wait()


def step_call(shares, upper, lower, groups):
    order, width = upper.shape
    count = groups * PAIR
    in_vmem = pl.BlockSpec(memory_space=pltpu.VMEM)
    return pl.pallas_call(
        functools.partial(step_kernel, groups),
        out_shape=(jax.ShapeDtypeStruct(upper.shape, jnp.float32),) * 2,
        in_specs=[in_vmem] * (len(shares) + 2),
        out_specs=(pl.BlockSpec(memory_space=pl.ANY),) * 2,
        scratch_shapes=[pltpu.VMEM((order, order), jnp.bfloat16)] * 2
        + [pltpu.VMEM((order, width), jnp.float32)] * 2
        + [pltpu.SemaphoreType.DMA((2,))],
        compiler_params=pltpu.CompilerParams(vmem_limit_bytes=48 * 1024 * 1024),
    )(*shares, upper, lower)


def spread(share, moved, rows, row):
    def send(value, moves):
        pairs = []
        for first in range(0, rows, QUARTET):
            pairs += [(PAIR * (first + a) + x, PAIR * (first + b) + x) for a, b in moves for x in range(PAIR)]
        return lax.ppermute(value, "blk", pairs)

    assert rows % QUARTET == 0
    stride = QUARTET
    while stride < rows:
        stride *= 2
    while stride > QUARTET:
        stride //= 2
        heads = range(0, rows - stride, 2 * stride)
        pairs = [(PAIR * a + x, PAIR * (a + stride) + x) for a in heads for x in range(PAIR)]
        received = lax.ppermute(share, "blk", pairs)
        share = jnp.where(lax.rem(row, 2 * stride) == stride, received, share)
    place = lax.rem(row, QUARTET)
    top, bottom = jnp.split(share, 2, axis=0)
    top_one = send(top, [(0, 1), (1, 0), (2, 3), (3, 2)])
    bottom_two = send(bottom, [(0, 2)])
    holds = jnp.where(place == 1, top_one, jnp.where(place == 2, bottom_two, bottom))
    top_three = send(top_one, [(1, 3)])
    passed = send(holds, [(0, 1), (1, 2), (2, 3), (3, 0)])
    top_three, moved = lax.optimization_barrier((top_three, moved))
    top = jnp.where(place == 0, top, jnp.where(place == 1, top_one, jnp.where(place == 2, passed, top_three)))
    bottom = jnp.where(place == 0, bottom, jnp.where(place == 2, bottom_two, passed))
    return jnp.concatenate([top, bottom], axis=0), moved


def exchange(share, rows, groups):
    size = groups * PAIR
    shares = []
    for flip in range(PAIR):
        for step in range(groups):
            sends = [
                (
                    (PAIR * row + (x ^ flip)) * size + (y + step) % groups * PAIR + core,
                    (PAIR * row + x) * size + y * PAIR + core,
                )
                for row in range(rows)
                for x in range(PAIR)
                for y in range(groups)
                for core in range(PAIR)
            ]
            mine = lax.ppermute(share, ("blk", "col"), sends) if flip or step else share
            swap = [(column, column ^ 1) for column in range(size)]
            shares += [mine, lax.ppermute(mine, "col", swap)]
    return shares


def shards(upper_row, lower_row):
    blocks, size = lax.axis_size("blk"), lax.axis_size("col")
    assert upper_row.shape[1] == 1 and blocks % PAIR == 0 and size % PAIR == 0
    rows, groups = blocks // PAIR, size // PAIR
    block = lax.axis_index("blk")
    upper, lower = upper_row[:, 0, :], lower_row[:, 0, :]
    side = lax.rem(block, PAIR)
    swapped = lax.ppermute(upper, "blk", [(source, source ^ 1) for source in range(blocks)])
    share = jnp.where(side == 0, upper, lower)
    share, swapped = spread(share, swapped, rows, block // PAIR)
    ahead = [(source, source + PAIR) for source in range(0, blocks - PAIR, PAIR)]
    shifted = jnp.where(side == 1, swapped, lax.ppermute(swapped, "blk", ahead))
    shares = exchange(share, rows, groups)
    new_upper, new_lower = step_call(shares, shifted, lower, groups)
    return new_upper[:, None, :], new_lower[:, None, :]


def solution(mesh):
    placement = P(None, "blk", "col")
    return jax.shard_map(
        shards,
        mesh=mesh,
        in_specs=(placement, placement),
        out_specs=(placement, placement),
        check_vma=False,
    )
```

```python
import functools

import jax
import jax.numpy as jnp
from jax import lax
from jax.experimental import pallas as pl
from jax.experimental.pallas import tpu as pltpu
from jax.sharding import PartitionSpec as P

PAIR = 2
QUARTET = 4
LEAD = 4.0


def halves(value):
    high = value.astype(jnp.bfloat16)
    return high, (value - high.astype(jnp.float32)).astype(jnp.bfloat16)


def dot(left, right, side):
    return lax.dot_general(left, right, (((1,), (side,)), ((), ())), preferred_element_type=jnp.float32)


def product(left, right, side=0):
    (left_high, left_low), (right_high, right_low) = left, right
    return dot(
        jnp.concatenate([left_high, left_high, left_low], axis=1),
        jnp.concatenate([right_high, right_low, right_high], axis=side),
        side,
    )


def thin_product(left, right, side=0):
    (left_high, left_low), (right_high, right_low) = halves(left), right
    both = dot(jnp.concatenate([left_high, left_low], axis=0), right_high, side)
    return both[: left.shape[0]] + both[left.shape[0] :] + dot(left_high, right_low, side)


def step_kernel(groups, *refs):
    count = groups * PAIR
    shares = refs[: PAIR * count]
    upper_ref, lower_ref, new_upper_ref, new_lower_ref = refs[PAIR * count : PAIR * count + 4]
    rest_high, rest_low, made_upper, made_lower, sent = refs[PAIR * count + 4 :]
    order, width = upper_ref.shape
    block, here = lax.axis_index("blk"), lax.axis_index("col")
    on_upper = lax.rem(block, PAIR) == 0
    square_shape = (width, width)
    unit = jnp.where(
        lax.broadcasted_iota(jnp.int32, square_shape, 0) == lax.broadcasted_iota(jnp.int32, square_shape, 1), 1.0, 0.0
    )
    rows = []
    for step in range(groups):
        for side in range(PAIR):
            column = lax.rem(here // PAIR + step, groups) * PAIR + lax.rem(here + side, PAIR)
            rows.append(pl.ds(pl.multiple_of(column * width, width), width))
    total = jnp.zeros((8, width), jnp.float32)
    for i in range(count):
        columns = slice(i * width, (i + 1) * width)
        for j in range(count):
            head = jnp.where(on_upper, shares[i][rows[j], :], shares[count + i][rows[j], :])
            total = total + jnp.sum((head * head).reshape(-1, 8, width), axis=0)
            to = slice(j * width, (j + 1) * width)
            rest_high[to, columns], rest_low[to, columns] = halves(head - LEAD * unit if i == j else head)
    scale = lax.rsqrt(jnp.full((1, 1), jnp.sum(total)) / order + 1e-06)
    shift = 1.0 - LEAD * scale
    rest = (rest_high[...], rest_low[...])
    strips = []
    for first in range(0, order, order // 2):
        strip = slice(first, first + order // 2)
        parts = [jnp.where(on_upper, shares[count + i][strip, :], shares[i][strip, :]) for i in range(count)]
        strips.append(jnp.concatenate(parts, axis=1))
    powers, sums = strips, strips
    for _ in range(3):
        powers = [shift * power - scale * thin_product(power, rest) for power in powers]
        sums = [total + power for total, power in zip(sums, powers)]
    reflects = [halves(total * scale) for total in sums]
    reflect = tuple(jnp.concatenate(parts, axis=0) for parts in zip(*reflects))
    upper = jnp.concatenate([upper_ref[part, :].T for part in rows], axis=1)
    lower = lower_ref[...].T
    gram = halves(product(reflect, reflect, 1))
    bent = thin_product(upper, reflect, 1)
    pulled = thin_product(lower, gram)
    bases = [bent - pulled, pulled - thin_product(bent, gram)]
    inners = [0.3125 * base + 0.0625 * thin_product(base, gram) for base in bases]
    inners = [0.375 * base + thin_product(inner, gram) for base, inner in zip(bases, inners)]
    inner_upper, inner_lower = [0.5 * base + thin_product(inner, gram) for base, inner in zip(bases, inners)]
    made_lower[...] = (lower - bent + inner_lower).T
    lower_copy = pltpu.make_async_copy(made_lower, new_lower_ref, sent.at[0])
    lower_copy.start()
    copies = [lower_copy]
    upper = upper - thin_product(lower - inner_upper, reflect)
    for i, part in enumerate(rows):
        made_upper[part, :] = upper[:, i * width : (i + 1) * width].T
        copy = pltpu.make_async_copy(made_upper.at[part, :], new_upper_ref.at[part, :], sent.at[1 + i])
        copy.start()
        copies.append(copy)
    for copy in copies:
        copy.wait()


def step_call(shares, upper, lower, groups):
    order, width = upper.shape
    count = groups * PAIR
    in_vmem = pl.BlockSpec(memory_space=pltpu.VMEM)
    return pl.pallas_call(
        functools.partial(step_kernel, groups),
        out_shape=(jax.ShapeDtypeStruct(upper.shape, jnp.float32),) * 2,
        in_specs=[in_vmem] * (len(shares) + 2),
        out_specs=(pl.BlockSpec(memory_space=pl.ANY),) * 2,
        scratch_shapes=[pltpu.VMEM((order, order), jnp.bfloat16)] * 2
        + [pltpu.VMEM((order, width), jnp.float32)] * 2
        + [pltpu.SemaphoreType.DMA((1 + count,))],
        compiler_params=pltpu.CompilerParams(vmem_limit_bytes=48 * 1024 * 1024),
    )(*shares, upper, lower)


def spread(share, moved, rows, row):
    def send(value, moves):
        pairs = []
        for first in range(0, rows, QUARTET):
            pairs += [(PAIR * (first + a) + x, PAIR * (first + b) + x) for a, b in moves for x in range(PAIR)]
        return lax.ppermute(value, "blk", pairs)

    assert rows % QUARTET == 0
    stride = QUARTET
    while stride < rows:
        stride *= 2
    while stride > QUARTET:
        stride //= 2
        heads = range(0, rows - stride, 2 * stride)
        pairs = [(PAIR * a + x, PAIR * (a + stride) + x) for a in heads for x in range(PAIR)]
        received = lax.ppermute(share, "blk", pairs)
        share = jnp.where(lax.rem(row, 2 * stride) == stride, received, share)
    place = lax.rem(row, QUARTET)
    top, bottom = jnp.split(share, 2, axis=0)
    top_one = send(top, [(0, 1), (1, 0), (2, 3), (3, 2)])
    bottom_two = send(bottom, [(0, 2)])
    holds = jnp.where(place == 1, top_one, jnp.where(place == 2, bottom_two, bottom))
    top_three = send(top_one, [(1, 3)])
    passed = send(holds, [(0, 1), (1, 2), (2, 3), (3, 0)])
    top_three, moved = lax.optimization_barrier((top_three, moved))
    top = jnp.where(place == 0, top, jnp.where(place == 1, top_one, jnp.where(place == 2, passed, top_three)))
    bottom = jnp.where(place == 0, bottom, jnp.where(place == 2, bottom_two, passed))
    return jnp.concatenate([top, bottom], axis=0), moved


def exchange(share, rows, groups):
    size = groups * PAIR
    shares = []
    for flip in range(PAIR):
        for step in range(groups):
            sends = [
                (
                    (PAIR * row + (x ^ flip)) * size + (y + step) % groups * PAIR + core,
                    (PAIR * row + x) * size + y * PAIR + core,
                )
                for row in range(rows)
                for x in range(PAIR)
                for y in range(groups)
                for core in range(PAIR)
            ]
            mine = lax.ppermute(share, ("blk", "col"), sends) if flip or step else share
            swap = [(column, column ^ 1) for column in range(size)]
            shares += [mine, lax.ppermute(mine, "col", swap)]
    return shares


def shards(upper_row, lower_row):
    blocks, size = lax.axis_size("blk"), lax.axis_size("col")
    assert upper_row.shape[1] == 1 and blocks % PAIR == 0 and size % PAIR == 0
    rows, groups = blocks // PAIR, size // PAIR
    block = lax.axis_index("blk")
    upper, lower = upper_row[:, 0, :], lower_row[:, 0, :]
    side = lax.rem(block, PAIR)
    swapped = lax.ppermute(upper, "blk", [(source, source ^ 1) for source in range(blocks)])
    share = jnp.where(side == 0, upper, lower)
    share, swapped = spread(share, swapped, rows, block // PAIR)
    ahead = [(source, source + PAIR) for source in range(0, blocks - PAIR, PAIR)]
    shifted = jnp.where(side == 1, swapped, lax.ppermute(swapped, "blk", ahead))
    shares = exchange(share, rows, groups)
    new_upper, new_lower = step_call(shares, shifted, lower, groups)
    return new_upper[:, None, :], new_lower[:, None, :]


def solution(mesh):
    placement = P(None, "blk", "col")
    return jax.shard_map(
        shards,
        mesh=mesh,
        in_specs=(placement, placement),
        out_specs=(placement, placement),
        check_vma=False,
    )
```
